32 devices in a mesh: members: 2 (over y), gx: 4 (over z), gy: 2 (over x), wa: 2 (over core).
Axes of the slice: x: 2, y: 2, z: 4, core: 2. Of those that a mesh axis runs over, the one named last changes fastest.
Arguments:
- adjoint: float32 [3, 128, 32, 256], P(None, ('members', 'gx'), 'gy', 'wa'), parts along dimension 1, may hold values from -6 to 6
- permeability: float32 [3, 128, 32, 256], P(None, ('members', 'gx'), 'gy', 'wa'), parts along dimension 1, may hold values from 0.1 to 10
- pore_volume: float32 [128, 32, 256], P(('members', 'gx'), 'gy', 'wa'), parts along dimension 0, may hold values from 0.05 to 0.5
- rock_type: int32 [128, 32, 256], P(('members', 'gx'), 'gy', 'wa'), parts along dimension 0, may hold values from 0 to 7
- rock_table: float32 [8, 3], replicated, may hold values from 0.2 to 2
- perf_column: int32 [1024], P(('gx', 'gy')), may hold values from 0 to 255
- perf_owner: int32 [1024, 1], P(('gx', 'gy')), may hold values from 0 to 7; in each aligned block of 128 rows (0 to 127, 128 to 255, ...) at most 32 rows name the same one
- perf_slot: int32 [1024], P(('gx', 'gy')), may hold values from 0 to 7
- observed: float32 [64, 256], P(('gx', 'gy'), 'wa'), may hold values from -4 to 4
Outputs:
- adjoint_out: float32 [3, 128, 32, 256], P(None, ('members', 'gx'), 'gy', 'wa'), parts along dimension 1
- well_sens: float32 [128, 256], P(('members', 'gx', 'gy'), 'wa'), parts along dimension 0
The draws below stay inside these ranges and needn't reach their ends.
There are 2 independent parts, one for each index of `members`. The reference program is written for one: setup_inputs(seed, part) draws one part's arguments, and reference() takes and returns one part's arrays. A program takes and returns all parts, laid end to end along the dimension named above; an argument that names none is the same for every part. Nothing has to cross between parts.
Inputs may be any that keep to these rules, and one draw needn't show every extreme that they name: `perf_owner`: within the rows of one grid block (aligned blocks of 128 rows) no value appears more than 32 times, and some value appears exactly 32 times.
All inputs are finite; a program needn't handle non-finite values.
Results may differ from the reference program's by a relative error of at most 0.0001.
Values sent between devices are 32-bit elements; how exact they have to be, the bound alone decides.
No kernel may reach another device: no remote copies, remote signals or barrier semaphores. Data moves between devices by JAX's collectives and lax.ppermute only.
A program may use at most 64 MiB of HBM per device.

```python
import math
import jax
import jax.numpy as jnp
import numpy as np
from jax import lax

CX = 16
CY = 16
PERF_DEV = 128
WELLS_DEV = 8
ROCKS = 8
STEPS = 4
NX = 64
NY = 32
NZ = 256
OWNERS = 8
ROWS = 1024
WELLS = 64
CAP = 32
N_GY = 2


def plant(array, own_key, smallest, top_value):
    shape = array.shape
    place = [jax.random.randint(jax.random.fold_in(own_key, axis), (), 0, shape[axis]) for axis in range(len(shape))]
    array = array.at[tuple(place)].set(smallest)
    longest = shape.index(max(shape))
    place[longest] = (place[longest] + 1) % shape[longest]
    return array.at[tuple(place)].set(top_value)


def block_levels(key, extent, cuts, smallest, largest):
    def one(position, parts):
        steps = jax.random.uniform(jax.random.fold_in(jax.random.fold_in(key, 6), position), (parts,), jnp.float32, smallest / len(cuts), largest / len(cuts))
        return jnp.repeat(jnp.exp(steps), extent[position] // parts).reshape((-1,) + (1,) * (len(extent) - position - 1))

    gain = one(*cuts[0])
    for cut in cuts[1:]:
        gain = gain * one(*cut)
    return gain


def deal_out(own_key, own, number, rows, count, top, limit, slope):
    ranking = jax.random.permutation(own_key, count)
    heavy_load, usual = load_shares(count, rows * top, limit, slope, True), load_shares(count, rows * top, limit, slope, False)
    places = jnp.arange(count)

    def named(lengths, rotation):
        used = int((lengths > 0).sum())
        fixed = max(1, used // 4)
        moved = fixed + (places - fixed + rotation * (used - fixed)) % max(1, count - fixed)
        return jnp.zeros((count,), jnp.int32).at[ranking[jnp.where(places < fixed, places, moved)]].set(jnp.asarray(lengths, jnp.int32))

    lengths = jnp.where(number % 4 == 0, named(heavy_load, number // 4), named(usual, number - number // 4 - 1))
    mixed = jax.random.permutation(jax.random.fold_in(own, 3), count)
    giver, taker = mixed[0:count // 2 * 2:2], mixed[1:count // 2 * 2:2]
    margin = jnp.minimum(lengths[giver] - 1, limit - lengths[taker]) // 2
    margin = jnp.where((giver == ranking[0]) | (taker == ranking[0]) | (lengths[taker] == 0), 0, jnp.maximum(margin, 0))
    moved = jax.random.randint(jax.random.fold_in(own, 4), (count // 2,), 0, 1 << 20) % (margin + 1)
    lengths = lengths.at[giver].add(-moved).at[taker].add(moved)
    items = jnp.searchsorted(jnp.cumsum(lengths), jnp.arange(rows * top), side="right").astype(jnp.int32)
    listing = items.reshape(top, rows).T
    listing = listing[jax.random.permutation(jax.random.fold_in(own, 1), rows)]
    rotation = jax.random.randint(jax.random.fold_in(own, 2), (rows, 1), 0, top)
    return jnp.take_along_axis(listing, (jnp.arange(top)[None, :] + rotation) % top, axis=1)


def load_shares(amount, total, most, slope, full):
    weights = [(1 << 20) // math.isqrt(rank ** slope) + 1 for rank in range(1, amount + 1)]
    largest = most if full else min(most, max(-(-total // amount), total * weights[0] // sum(weights)))
    least = 1 if total - largest >= amount - 1 else 0
    given, rest = [largest] + [least] * (amount - 1), total - largest - least * (amount - 1)
    while rest > 0:
        candidates = [i for i in range(1, amount) if given[i] < largest] or [i for i in range(1, amount) if given[i] < most]
        pool, budget = sum([weights[i] for i in candidates]), rest
        for i in candidates:
            extra = min(most - given[i], max(1, budget * weights[i] // pool), rest)
            given[i] = given[i] + extra
            rest = rest - extra
    return np.array(given)


def gaussian(stream_key, dims, spread, reach, cuts=(), kind=jnp.bfloat16):
    level = block_levels(stream_key, dims, cuts, -0.22, 0.18) if cuts else 1.0
    result = jax.random.normal(stream_key, dims, jnp.float32) * spread * level
    return jnp.minimum(jnp.maximum(result, -reach), reach).astype(kind)


def setup_inputs(seed: int = 0, part: int = 0) -> dict:
    seeds = jax.random.split(jax.random.key(seed), 10)
    own_keys = jax.random.split(jax.random.fold_in(seeds[9], part), 10)
    adjoint = gaussian(own_keys[0], (3, NX, NY, NZ), 1.0, 6.0, ((1, 4), (2, 2), (3, 2)), jnp.float32)
    permeability = jnp.clip(jnp.exp(math.log(10.0) - 4.6051702 * jax.random.uniform(own_keys[1], (3, NX, NY, NZ), jnp.float32) ** block_levels(own_keys[1], (3, NX, NY, NZ), ((1, 4), (2, 2), (3, 2)), -0.2, 0.2)), 0.1, 10.0)
    pore_volume = jnp.clip(jnp.exp(math.log(0.5) - 2.3025851 * jax.random.uniform(own_keys[2], (NX, NY, NZ), jnp.float32) ** block_levels(own_keys[2], (NX, NY, NZ), ((0, 4), (1, 2), (2, 2)), -0.2, 0.2)), 0.05, 0.5)
    rock_type = plant(jax.random.randint(own_keys[3], (NX, NY, NZ), 0, ROCKS), jax.random.fold_in(own_keys[3], 1), 0, ROCKS - 1).astype(jnp.int32)
    rock_table = jnp.clip(jnp.exp(jax.random.uniform(seeds[4], (ROCKS, 3), jnp.float32, math.log(0.2), math.log(2.0))), 0.2, 2.0)
    perf_column = plant(jax.random.randint(seeds[5], (ROWS,), 0, CX * CY), jax.random.fold_in(seeds[5], 1), 0, (CX * CY) - 1).astype(jnp.int32)
    perf_owner_keys = jax.random.split(jax.random.fold_in(seeds[6], 1), ROWS // PERF_DEV)
    perf_owner_turns = jax.random.permutation(jax.random.fold_in(seeds[6], 3), ROWS // PERF_DEV)
    perf_owner = jax.vmap(lambda own, number: deal_out(jax.random.fold_in(seeds[6], 2), own, number, PERF_DEV, OWNERS, 1, CAP, 2))(perf_owner_keys, perf_owner_turns).reshape((ROWS, 1))
    perf_slot = plant(jax.random.randint(seeds[7], (ROWS,), 0, WELLS_DEV), jax.random.fold_in(seeds[7], 1), 0, WELLS_DEV - 1).astype(jnp.int32)
    observed = gaussian(seeds[8], (WELLS, NZ), 1.0, 4.0, ((0, 8), (1, 2)), jnp.float32)
    return {"adjoint": adjoint, "permeability": permeability, "pore_volume": pore_volume, "rock_type": rock_type, "rock_table": rock_table, "perf_column": perf_column, "perf_owner": perf_owner, "perf_slot": perf_slot, "observed": observed}


def harmonic(first, second):
    return 2.0 * first * second / (first + second)

def reference(adjoint, permeability, pore_volume, rock_type, rock_table, perf_column, perf_owner, perf_slot, observed):
    padded_perm = jnp.pad(permeability, ((0, 0), (1, 1), (1, 1), (1, 1)))
    t_xm = harmonic(permeability[0], padded_perm[0, :-2, 1:-1, 1:-1])
    t_xp = harmonic(permeability[0], padded_perm[0, 2:, 1:-1, 1:-1])
    t_ym = harmonic(permeability[1], padded_perm[1, 1:-1, :-2, 1:-1])
    t_yp = harmonic(permeability[1], padded_perm[1, 1:-1, 2:, 1:-1])
    t_zm = harmonic(permeability[2], padded_perm[2, 1:-1, 1:-1, :-2])
    t_zp = harmonic(permeability[2], padded_perm[2, 1:-1, 1:-1, 2:])
    weight_sum = t_xm + t_xp + t_ym + t_yp + t_zm + t_zp
    mobility = jnp.moveaxis(jnp.take(rock_table, rock_type, axis=0), -1, 0)
    root_perm = jnp.sqrt(permeability[0] * permeability[1])
    well_index = root_perm / (1.0 + root_perm)
    row_ids = jnp.arange(ROWS, dtype=jnp.int32)
    block_ids = row_ids // PERF_DEV
    x_cols = block_ids // N_GY * CX + perf_column // CY
    y_cols = block_ids % N_GY * CY + perf_column % CY
    column_ids = (x_cols * NY + y_cols).astype(jnp.int32)
    well_ids = (perf_owner[:, 0] * WELLS_DEV + perf_slot).astype(jnp.int32)
    well_sens = jnp.zeros((WELLS, NZ), jnp.float32)
    for iteration in range(STEPS):
        combined = well_index * lax.optimization_barrier(jnp.sum(mobility * adjoint, axis=0)) / 4.0
        flow = jnp.take(combined.reshape(NX * NY, NZ), column_ids, axis=0)
        well_sens = jax.ops.segment_sum(flow, well_ids, num_segments=WELLS)
        response = jnp.tanh(well_sens - observed)
        back = jnp.take(response, well_ids, axis=0)
        column_sum = jax.ops.segment_sum(back, column_ids, num_segments=NX * NY).reshape(NX, NY, NZ)
        source = well_index[None] * mobility * column_sum[None]
        padded = jnp.pad(adjoint, ((0, 0), (1, 1), (1, 1), (1, 1)))
        beside = t_xm * padded[:, :-2, 1:-1, 1:-1] + t_xp * padded[:, 2:, 1:-1, 1:-1]
        beside = beside + t_ym * padded[:, 1:-1, :-2, 1:-1] + t_yp * padded[:, 1:-1, 2:, 1:-1]
        beside = beside + t_zm * padded[:, 1:-1, 1:-1, :-2] + t_zp * padded[:, 1:-1, 1:-1, 2:]
        adjoint = (pore_volume * adjoint + mobility * beside + source) / (pore_volume + mobility * weight_sum)
    return (adjoint, well_sens)
```

```python
import functools

import jax
import jax.numpy as jnp
from jax import lax
from jax.experimental import pallas as pl
from jax.experimental.pallas import tpu as pltpu
from jax.sharding import PartitionSpec as P

STEPS = 4
F32 = jnp.float32
BF16 = jnp.bfloat16
VMEM = pl.BlockSpec(memory_space=pltpu.VMEM)
SMEM = pl.BlockSpec(memory_space=pltpu.SMEM)
XM, XP, YM, YP, ZM, ZP, Y_ODD, X_ODD, OWNER = range(9)


def harmonic(first, second):
    return 2.0 * first * second / (first + second)


def split(value):
    high = value.astype(BF16)
    rest = value - high.astype(F32)
    middle = rest.astype(BF16)
    low = (rest - middle.astype(F32)).astype(BF16)
    return jnp.concatenate([high, middle, low], axis=1)


def counted(counts, value):
    n = value.shape[1]
    out = jnp.dot(counts, split(value), preferred_element_type=F32)
    return out[:, :n] + (out[:, n : 2 * n] + out[:, 2 * n :])


def start_kernel(
    info, table, adj, perm, rock, column, well, observed,
    mob, index, gain, counts, counts_t, target, msg_y, face_a, face_b, msg_z, combined,
):
    _, nx, ny, nz = adj.shape
    rocks = table.shape[0]
    wells = target.shape[0]
    own = observed.shape[0]
    rows = column.shape[1]
    y_odd = info[Y_ODD] == 1
    x_odd = info[X_ODD] == 1
    well_hit = (lax.broadcasted_iota(jnp.int32, (wells, rows), 0) == well[...]).astype(BF16)
    col_hit = (lax.broadcasted_iota(jnp.int32, (nx * ny, rows), 0) == column[...]).astype(BF16)
    contract = (((1,), (1,)), ((), ()))
    count = lax.dot_general(well_hit, col_hit, contract, preferred_element_type=F32).astype(BF16)
    counts[...] = count
    counts_t[...] = lax.dot_general(
        col_hit, well_hit, contract, preferred_element_type=F32
    ).astype(BF16)
    target[...] = jnp.zeros_like(target)
    target[pl.ds(pl.multiple_of(info[OWNER] * own, own), own), :] = observed[...]
    for x in range(nx):
        kind = rock[x]
        root = jnp.sqrt(perm[0, x] * perm[1, x])
        wi = root / (1.0 + root)
        index[x] = wi
        total = jnp.zeros((ny, nz), F32)
        for p in range(3):
            m = jnp.full((ny, nz), table[0, p], F32)
            for r in range(1, rocks):
                m = jnp.where(kind == r, table[r, p], m)
            mob[p, x] = m
            g = 0.25 * wi * m
            gain[p, x] = g
            total = total + g * adj[p, x]
            msg_z[p, x] = adj[p, x]
            row = wells + p * nx + x
            msg_y[row : row + 1, :] = jnp.where(
                y_odd, adj[p, x, 0:1, :], adj[p, x, ny - 1 : ny, :]
            )
        msg_z[3, x] = perm[2, x]
        row = wells + 3 * nx + x
        msg_y[row : row + 1, :] = jnp.where(
            y_odd, perm[1, x, 0:1, :], perm[1, x, ny - 1 : ny, :]
        )
        combined[x * ny : (x + 1) * ny, :] = total
    for p in range(4):
        low = adj[p, 0] if p < 3 else perm[0, 0]
        high = adj[p, nx - 1] if p < 3 else perm[0, nx - 1]
        face_a[p * ny : (p + 1) * ny, :] = jnp.where(x_odd, low, high)
        face_b[p * ny : (p + 1) * ny, :] = jnp.where(x_odd, high, low)
    msg_y[0:wells, :] = counted(count, combined[...]) - target[...]


def sweep_kernel(first, last, refs_in, *refs):
    names = refs_in
    r = dict(zip(names, refs))
    info, adj = r["info"], r["adj"]
    _, nx, ny, nz = adj.shape
    wells = r["target"].shape[0]
    y_odd = info[Y_ODD] == 1
    x_odd = info[X_ODD] == 1
    total = r["sum0"][...]
    for name in names:
        if name.startswith("more"):
            total = total + r[name][0:wells, :]
    column_sum = counted(r["counts_t"][...], jnp.tanh(total))
    lane = lax.broadcasted_iota(jnp.int32, (ny, nz), 1)
    sub = lax.broadcasted_iota(jnp.int32, (ny, nz), 0)
    at_first, at_last = lane == 0, lane == nz - 1
    top, bottom = sub == 0, sub == ny - 1

    y0 = r["ym"].shape[0] - (4 if first else 3) * nx
    x0 = r["xm"].shape[0] - (4 if first else 3) * ny

    def y_minus(value, p, x):
        edge = r["ym"][y0 + p * nx + x : y0 + p * nx + x + 1, :]
        return jnp.where(top, edge, pltpu.roll(value, 1, 0))

    def y_plus(value, p, x):
        edge = r["yp"][y0 + p * nx + x : y0 + p * nx + x + 1, :]
        return jnp.where(bottom, edge, pltpu.roll(value, ny - 1, 0))

    def z_minus(value, p, x):
        return pltpu.roll(jnp.where(at_last, r["zm"][p, x], value), 1, 1)

    def z_plus(value, p, x):
        return pltpu.roll(jnp.where(at_first, r["zp"][p, x], value), nz - 1, 1)

    def x_face(name, p):
        return r[name][x0 + p * ny : x0 + (p + 1) * ny, :]

    for x in range(nx):
        if first:
            perm = r["perm"]
            k = perm[0, x]
            km = perm[0, x - 1] if x else jnp.where(info[XM] == 1, x_face("xm", 3), 0.0)
            kp = perm[0, x + 1] if x < nx - 1 else jnp.where(info[XP] == 1, x_face("xp", 3), 0.0)
            txm, txp = harmonic(k, km), harmonic(k, kp)
            k = perm[1, x]
            km, kp = y_minus(k, 3, x), y_plus(k, 3, x)
            tym = harmonic(k, jnp.where(top & (info[YM] == 0), 0.0, km))
            typ = harmonic(k, jnp.where(bottom & (info[YP] == 0), 0.0, kp))
            k = perm[2, x]
            km, kp = z_minus(k, 3, x), z_plus(k, 3, x)
            tzm = harmonic(k, jnp.where(at_first & (info[ZM] == 0), 0.0, km))
            tzp = harmonic(k, jnp.where(at_last & (info[ZP] == 0), 0.0, kp))
            weights = (txm, txp, tym, typ, tzm, tzp)
            for f, t in enumerate(weights):
                r["t_out"][f, x] = t
            weight_sum = txm + txp + tym + typ + tzm + tzp
            pore = r["pore"][x]
        else:
            weights = tuple(r["t"][f, x] for f in range(6))
        txm, txp, tym, typ, tzm, tzp = weights
        well_term = r["index"][x] * column_sum[x * ny : (x + 1) * ny, :]
        flow = jnp.zeros((ny, nz), F32)
        for p in range(3):
            if first:
                m = r["mob"][p, x]
                inverse = 1.0 / (pore + m * weight_sum)
                keep, take = pore * inverse, m * inverse
                r["keep_out"][p, x] = keep
                r["take_out"][p, x] = take
            else:
                keep, take = r["keep"][p, x], r["take"][p, x]
            value = adj[p, x]
            before = adj[p, x - 1] if x else x_face("xm", p)
            after = adj[p, x + 1] if x < nx - 1 else x_face("xp", p)
            beside = txm * before + txp * after
            beside = beside + tym * y_minus(value, p, x) + typ * y_plus(value, p, x)
            beside = beside + tzm * z_minus(value, p, x) + tzp * z_plus(value, p, x)
            new = keep * value + take * (beside + well_term)
            r["new"][p, x] = new
            if not last:
                flow = flow + r["gain"][p, x] * new
                row = wells + p * nx + x
                r["msg_y"][row : row + 1, :] = jnp.where(
                    y_odd, new[0:1, :], new[ny - 1 : ny, :]
                )
                if x == 0:
                    low = new
                    r["face_lo"][p * ny : (p + 1) * ny, :] = low
                if x == nx - 1:
                    low = r["face_lo"][p * ny : (p + 1) * ny, :]
                    r["face_a"][p * ny : (p + 1) * ny, :] = jnp.where(x_odd, low, new)
                    r["face_b"][p * ny : (p + 1) * ny, :] = jnp.where(x_odd, new, low)
        if not last:
            r["combined"][x * ny : (x + 1) * ny, :] = flow
    if last:
        sens = r["sens"]
        own = sens.shape[0]
        at = pl.ds(pl.multiple_of(info[OWNER] * own, own), own)
        summed = r["sum0"][at, :]
        for name in names:
            if name.startswith("more"):
                summed = summed + r[name][at, :]
        sens[...] = summed + r["target"][at, :]
    else:
        r["msg_y"][0:wells, :] = counted(r["counts"][...], r["combined"][...]) - r["target"][...]


def call(kernel, ins, outs, scratch):
    return pl.pallas_call(
        kernel,
        in_specs=[SMEM if smem else VMEM for smem, _ in ins],
        out_specs=[VMEM] * len(outs),
        out_shape=[jax.ShapeDtypeStruct(shape, kind) for shape, kind in outs],
        scratch_shapes=scratch,
        compiler_params=pltpu.CompilerParams(vmem_limit_bytes=40 * 1024 * 1024),
    )(*[array for _, array in ins])


def swap(count, bit):
    return [(i, i ^ bit) for i in range(count)]


def neighbours(low, high, axis):
    count = lax.axis_size(axis)
    before = lax.ppermute(high, axis, [(i, i + 1) for i in range(count - 1)])
    after = lax.ppermute(low, axis, [(i + 1, i) for i in range(count - 1)])
    return before, after


def summed_over(value, axis):
    count = lax.axis_size(axis)
    if count & (count - 1):
        return lax.psum(value, axis)
    bit = 1
    while bit < count:
        value = value + lax.ppermute(value, axis, swap(count, bit))
        bit *= 2
    return value


def exchange(msg_y, face_a, face_b, block, edges, wells, x_odd):
    size_x, size_y, size_z = (lax.axis_size(a) for a in ("gx", "gy", "wa"))
    if size_z == 2:
        zm = zp = lax.ppermute(block, "wa", swap(2, 1))
    else:
        zm, zp = neighbours(block, block, "wa")
    if size_y == 2:
        ym = yp = lax.ppermute(msg_y, "gy", swap(2, 1))
        total = msg_y[:wells] + ym[:wells]
    else:
        ym, yp = neighbours(*edges("y"), "gy")
        total = summed_over(msg_y[:wells], "gy")
    if size_x == 4:
        one = lax.ppermute(jnp.concatenate([total, face_a]), "gx", swap(4, 1))
        ring = lax.ppermute(jnp.concatenate([total, face_b]), "gx", swap(4, 3))
        two = lax.ppermute(total, "gx", swap(4, 2))
        sums = (total, one, ring, two)
        xm = jnp.where(x_odd, one[wells:], ring[wells:])
        xp = jnp.where(x_odd, ring[wells:], one[wells:])
    else:
        xm, xp = neighbours(*edges("x"), "gx")
        sums = (summed_over(total, "gx"),)
    return sums, xm, xp, ym, yp, zm, zp


def local(
    adjoint, permeability, pore_volume, rock_type, rock_table,
    perf_column, perf_owner, perf_slot, observed,
):
    size_x, size_y, size_z = (lax.axis_size(a) for a in ("gx", "gy", "wa"))
    gx, gy, wa = (lax.axis_index(a) for a in ("gx", "gy", "wa"))
    _, nx, ny, nz = adjoint.shape
    rows = perf_column.shape[0]
    own = observed.shape[0]
    wells = own * size_x * size_y
    cells = (nx, ny, nz)
    x_odd = gx % 2
    info = jnp.stack(
        [gx > 0, gx < size_x - 1, gy > 0, gy < size_y - 1, wa > 0, wa < size_z - 1,
         gy % 2, x_odd, gx * size_y + gy]
    ).astype(jnp.int32)
    well = perf_owner[:, 0] * own + perf_slot
    outs = [
        ((3,) + cells, F32), (cells, F32), ((3,) + cells, F32),
        ((wells, nx * ny), BF16), ((nx * ny, wells), BF16), ((wells, nz), F32),
        ((wells + 4 * nx, nz), F32), ((4 * ny, nz), F32), ((4 * ny, nz), F32),
        ((4,) + cells, F32),
    ]
    ins = [
        (True, info), (True, rock_table), (False, adjoint), (False, permeability),
        (False, rock_type), (False, perf_column.reshape(1, rows)),
        (False, well.reshape(1, rows)), (False, observed),
    ]
    mob, index, gain, counts, counts_t, target, msg_y, face_a, face_b, block = call(
        start_kernel, ins, outs, [pltpu.VMEM((nx * ny, nz), F32)]
    )

    def edges_of(parts_x, parts_y):
        def edges(axis):
            if axis == "x":
                return (
                    jnp.concatenate([a[0] for a in parts_x]),
                    jnp.concatenate([a[nx - 1] for a in parts_x]),
                )
            return (
                jnp.concatenate([a[:, 0] for a in parts_y]),
                jnp.concatenate([a[:, ny - 1] for a in parts_y]),
            )

        return edges

    phases = [adjoint[p] for p in range(3)]
    edges = edges_of(phases + [permeability[0]], phases + [permeability[1]])
    adj = adjoint
    for step in range(STEPS):
        first, last = step == 0, step == STEPS - 1
        sums, xm, xp, ym, yp, zm, zp = exchange(
            msg_y, face_a, face_b, block, edges, wells, x_odd == 1
        )
        ins = {"info": info, "adj": adj, "target": target, "counts_t": counts_t, "index": index}
        ins.update({("more%d" % i if i else "sum0"): s for i, s in enumerate(sums)})
        ins.update(xm=xm, xp=xp, ym=ym, yp=yp, zm=zm, zp=zp)
        if not last:
            ins.update(gain=gain, counts=counts)
        if first:
            ins.update(perm=permeability, pore=pore_volume, mob=mob)
        else:
            ins.update(t=weights, keep=keep, take=take)
        outs = {"new": ((3,) + cells, F32)}
        if last:
            outs["sens"] = ((own, nz), F32)
        else:
            outs["msg_y"] = ((wells + 3 * nx, nz), F32)
            outs["face_a"] = ((3 * ny, nz), F32)
            outs["face_b"] = ((3 * ny, nz), F32)
        if first:
            outs["t_out"] = ((6,) + cells, F32)
            outs["keep_out"] = ((3,) + cells, F32)
            outs["take_out"] = ((3,) + cells, F32)
        scratch = {} if last else {
            "combined": pltpu.VMEM((nx * ny, nz), F32),
            "face_lo": pltpu.VMEM((3 * ny, nz), F32),
        }
        names = tuple(ins) + tuple(outs) + tuple(scratch)
        result = call(
            functools.partial(sweep_kernel, first, last, names),
            [(name == "info", array) for name, array in ins.items()],
            list(outs.values()),
            list(scratch.values()),
        )
        result = dict(zip(outs, result))
        adj = block = result["new"]
        if first:
            weights, keep, take = (result[k] for k in ("t_out", "keep_out", "take_out"))
        if not last:
            msg_y, face_a, face_b = (result[k] for k in ("msg_y", "face_a", "face_b"))
            phases = [adj[p] for p in range(3)]
            edges = edges_of(phases, phases)
    return (adj, result["sens"])


def solution(mesh):
    cell = P(None, ("members", "gx"), "gy", "wa")
    flat = P(("members", "gx"), "gy", "wa")
    placed = (
        cell, cell, flat, flat, P(), P(("gx", "gy")), P(("gx", "gy"), None), P(("gx", "gy")),
        P(("gx", "gy"), "wa"),
    )
    return jax.shard_map(
        local,
        mesh=mesh,
        in_specs=placed,
        out_specs=(cell, P(("members", "gx", "gy"), "wa")),
        check_vma=False,
    )
```

```python
import functools

import jax
import jax.numpy as jnp
from jax import lax
from jax.experimental import pallas as pl
from jax.experimental.pallas import tpu as pltpu
from jax.sharding import PartitionSpec as P

STEPS = 4
F32 = jnp.float32
BF16 = jnp.bfloat16
VMEM = pl.BlockSpec(memory_space=pltpu.VMEM)
HBM = pl.BlockSpec(memory_space=pltpu.HBM)
SMEM = pl.BlockSpec(memory_space=pltpu.SMEM)
MIB = 1024 * 1024


class Refs(dict):
    __getattr__ = dict.__getitem__


def harmonic(first, second):
    return 2.0 * first * second / (first + second)


def split(value):
    high = value.astype(BF16)
    rest = value - high.astype(F32)
    middle = rest.astype(BF16)
    low = (rest - middle.astype(F32)).astype(BF16)
    return jnp.concatenate([high, middle, low], axis=1)


def counted(counts, value):
    n = value.shape[1]
    out = jnp.dot(counts, split(value), preferred_element_type=F32)
    return out[:, :n] + (out[:, n : 2 * n] + out[:, 2 * n :])


def odd(axis):
    return lax.rem(lax.axis_index(axis), 2) == 1


def own_rows(own):
    owner = lax.axis_index("gx") * lax.axis_size("gy") + lax.axis_index("gy")
    return pl.ds(pl.multiple_of(owner * own, own), own)


def hits(r, wells, own, columns):
    rows = r.column.shape[1]
    well = r.owner[...] * own + r.slot[...]
    well_hit = (lax.broadcasted_iota(jnp.int32, (wells, rows), 0) == well).astype(BF16)
    col_hit = lax.broadcasted_iota(jnp.int32, (columns, rows), 0) == r.column[...]
    return well_hit, col_hit.astype(BF16)


def pairs(first, second):
    out = lax.dot_general(
        first, second, (((1,), (1,)), ((), ())), preferred_element_type=F32
    )
    return out.astype(BF16)


def plane_mobility(r, x):
    kind = r.rock[x]
    root = jnp.sqrt(r.perm[0, x] * r.perm[1, x])
    index = root / (1.0 + root)
    mobility = []
    for p in range(3):
        m = jnp.full(kind.shape, r.table[p, 0], F32)
        for k in range(1, r.table.shape[1]):
            m = jnp.where(kind == k, r.table[p, k], m)
        mobility.append(m)
    return index, mobility


def send_y(r, row, value):
    ny = value.shape[0]
    r.msg_y[row : row + 1, :] = jnp.where(odd("gy"), value[0:1, :], value[ny - 1 : ny, :])


def send_x(r, p, low, high):
    ny = low.shape[0]
    r.face_a[p * ny : (p + 1) * ny, :] = jnp.where(odd("gx"), low, high)
    r.face_b[p * ny : (p + 1) * ny, :] = jnp.where(odd("gx"), high, low)


def first_kernel(names, *refs):
    r = Refs(zip(names, refs))
    moved = ("column", "owner", "slot", "observed", "perm", "rock", "adj")
    copies = {}
    for i, name in enumerate(moved):
        copies[name] = pltpu.make_async_copy(r[name + "_in"], r[name], r.sems.at[i])
        copies[name].start()
    _, nx, ny, nz = r.adj.shape
    own = r.observed.shape[0]
    wells = r.msg_y.shape[0] - 4 * nx
    for name in moved[:4]:
        copies[name].wait()
    well_hit, col_hit = hits(r, wells, own, nx * ny)
    counts = pairs(well_hit, col_hit)
    for name in moved[4:]:
        copies[name].wait()
    for x in range(nx):
        index, mobility = plane_mobility(r, x)
        total = jnp.zeros((ny, nz), F32)
        for p in range(3):
            total = total + mobility[p] * r.adj[p, x]
            send_y(r, wells + p * nx + x, r.adj[p, x])
        send_y(r, wells + 3 * nx + x, r.perm[1, x])
        r.combined[x * ny : (x + 1) * ny, :] = 0.25 * index * total
    for p in range(3):
        send_x(r, p, r.adj[p, 0], r.adj[p, nx - 1])
    send_x(r, 3, r.perm[0, 0], r.perm[0, nx - 1])
    r.msg_y[0:wells, :] = counted(counts, r.combined[...])
    r.msg_y[own_rows(own), :] = r.msg_y[own_rows(own), :] - r.observed[...]


def inner_kernel(first, last, names, *refs):
    r = Refs(zip(names, refs))
    _, nx, ny, nz = r.adj.shape
    lane = lax.broadcasted_iota(jnp.int32, (ny, nz), 1)
    sub = lax.broadcasted_iota(jnp.int32, (ny, nz), 0)
    at_first, at_last = lane == 0, lane == nz - 1
    top, bottom = sub == 0, sub == ny - 1
    y0 = r.ym.shape[0] - (4 if first else 3) * nx

    def y_minus(value, p, x):
        edge = r.ym[y0 + p * nx + x : y0 + p * nx + x + 1, :]
        return jnp.where(top, edge, pltpu.roll(value, 1, 0))

    def y_plus(value, p, x):
        edge = r.yp[y0 + p * nx + x : y0 + p * nx + x + 1, :]
        return jnp.where(bottom, edge, pltpu.roll(value, ny - 1, 0))

    def z_minus(value, beside):
        return pltpu.roll(jnp.where(at_last, beside, value), 1, 1)

    def z_plus(value, beside):
        return pltpu.roll(jnp.where(at_first, beside, value), nz - 1, 1)

    if first:
        own = r.observed.shape[0]
        wells = r.counts.shape[0]
        well_hit, col_hit = hits(r, wells, own, nx * ny)
        r.counts[...] = pairs(well_hit, col_hit)
        r.counts_t[...] = pairs(col_hit, well_hit)
        ends = {a: (lax.axis_index(a) == 0, lax.axis_index(a) == lax.axis_size(a) - 1)
                for a in ("gy", "wa")}
        zero = jnp.zeros((ny, nz), F32)
    for x in range(nx):
        edge = x in (0, nx - 1)
        if first:
            k = r.perm[0, x]
            txm = harmonic(k, r.perm[0, x - 1]) if x else zero
            txp = harmonic(k, r.perm[0, x + 1]) if x < nx - 1 else zero
            k = r.perm[1, x]
            tym = harmonic(k, jnp.where(top & ends["gy"][0], 0.0, y_minus(k, 3, x)))
            typ = harmonic(k, jnp.where(bottom & ends["gy"][1], 0.0, y_plus(k, 3, x)))
            k = r.perm[2, x]
            km, kp = z_minus(k, r.pm[2, x]), z_plus(k, r.pp[2, x])
            tzm = harmonic(k, jnp.where(at_first & ends["wa"][0], 0.0, km))
            tzp = harmonic(k, jnp.where(at_last & ends["wa"][1], 0.0, kp))
            weights = (txm, txp, tym, typ, tzm, tzp)
            for f, t in enumerate(weights):
                r.t[f, x] = t
            weight_sum = txm + txp + tym + typ + tzm + tzp
            r.weight[x] = weight_sum
            pore = r.pore[x]
            index, mobility = plane_mobility(r, x)
            r.index[x] = index
            reply = zero
        else:
            txm, txp, tym, typ, tzm, tzp = (r.t[f, x] for f in range(6))
        flow = jnp.zeros((ny, nz), F32)
        for p in range(3):
            value = r.adj[p, x]
            beside = tym * y_minus(value, p, x) + typ * y_plus(value, p, x)
            beside = beside + tzm * z_minus(value, r.zm[p, x])
            beside = beside + tzp * z_plus(value, r.zp[p, x])
            if x:
                beside = beside + txm * r.adj[p, x - 1]
            if x < nx - 1:
                beside = beside + txp * r.adj[p, x + 1]
            if first:
                m = mobility[p]
                gain = 0.25 * index * m
                r.gain[p, x] = gain
                if edge:
                    r.mob[p, 1 if x else 0] = m
                    r.base[p, x] = beside
                    continue
                inverse = 1.0 / (pore + m * weight_sum)
                keep, take = pore * inverse, m * inverse
                r.keep[p, x] = keep
                r.take[p, x] = take
                q = take * index
                r.q[p, x] = q
                reply = reply + gain * q
            elif edge:
                e = 1 if x else 0
                keep, take = r.edge_keep[p, e], r.edge_take[p, e]
            else:
                keep, take = r.keep[p, x], r.take[p, x]
            base = keep * value + take * beside
            r.base[p, x] = base
            if not last and not edge:
                flow = flow + r.gain[p, x] * base
        if not edge:
            if not last:
                r.flow[x] = flow
            if first:
                r.reply[x] = reply


def well_kernel(first, last, names, *refs):
    r = Refs(zip(names, refs))
    _, nx, ny, nz = r.base.shape
    wells = r.total.shape[0]
    total = r.total[...]
    for name in names:
        if name.startswith("more"):
            total = total + r[name][0:wells, :]
    if last:
        own = r.observed.shape[0]
        r.combined[...] = total
        r.sens[...] = r.combined[own_rows(own), :] + r.observed[...]
    column_sum = counted(r.counts_t[...], jnp.tanh(total))

    def x_face(p, e):
        if "xm" in r:
            return (r.xp if e else r.xm)[p * ny : (p + 1) * ny, :]
        at = slice(wells + p * ny, wells + (p + 1) * ny)
        one, ring = r.more1[at, :], r.more2[at, :]
        return jnp.where(odd("gx"), ring, one) if e else jnp.where(odd("gx"), one, ring)

    part = 4 if nx % 4 == 0 else 1
    copies = []
    gx, size_x = lax.axis_index("gx"), lax.axis_size("gx")
    for x in range(nx):
        edge = x in (0, nx - 1)
        e = 1 if x else 0
        wells_here = column_sum[x * ny : (x + 1) * ny, :]
        flow = None
        if edge:
            well_term = r.index[x] * wells_here
            if first:
                k = jnp.where(gx == (size_x - 1 if e else 0), 0.0, x_face(3, e))
                tx = harmonic(r.perm[0, x], k)
                r.edge_t[e] = tx
                weight_sum = r.weight[x] + tx
                pore = r.pore[x]
            else:
                tx = r.edge_t[e]
        for p in range(3):
            if not edge:
                new = r.base[p, x] + r.q[p, x] * wells_here
            elif first:
                m = r.mob[p, e]
                inverse = 1.0 / (pore + m * weight_sum)
                keep, take = pore * inverse, m * inverse
                r.edge_keep[p, e] = keep
                r.edge_take[p, e] = take
                beside = r.base[p, x] + tx * x_face(p, e)
                new = keep * r.adj[p, x] + take * (beside + well_term)
            else:
                new = r.base[p, x] + r.edge_take[p, e] * (tx * x_face(p, e) + well_term)
            if last:
                r.held[p, x] = new
                continue
            r.new[p, x] = new
            send_y(r, wells + p * nx + x, new)
            if edge:
                term = r.gain[p, x] * new
                flow = term if flow is None else flow + term
                if x:
                    send_x(r, p, r.new[p, 0], new)
        if last:
            if x % part == part - 1:
                at = pl.ds(x - part + 1, part)
                copies.append(
                    pltpu.make_async_copy(
                        r.held.at[:, at], r.new.at[:, at], r.sems.at[x // part]
                    )
                )
                copies[-1].start()
            continue
        if not edge:
            flow = r.flow[x] + r.reply[x] * wells_here
        r.combined[x * ny : (x + 1) * ny, :] = flow
    if last:
        for copy in copies:
            copy.wait()
    else:
        r.msg_y[0:wells, :] = counted(r.counts[...], r.combined[...])
        own = r.observed.shape[0]
        r.msg_y[own_rows(own), :] = r.msg_y[own_rows(own), :] - r.observed[...]


def call(kernel, ins, outs, scratch, limit=24, cost=None):
    names = tuple(ins) + tuple(outs) + tuple(scratch)
    result = pl.pallas_call(
        functools.partial(kernel, names),
        in_specs=[spec for spec, _ in ins.values()],
        out_specs=[spec for spec, _, _ in outs.values()],
        out_shape=[jax.ShapeDtypeStruct(shape, kind) for _, shape, kind in outs.values()],
        scratch_shapes=list(scratch.values()),
        compiler_params=pltpu.CompilerParams(vmem_limit_bytes=limit * MIB),
        cost_estimate=cost,
    )(*[array for _, array in ins.values()])
    return Refs(zip(outs, result))


def in_vmem(**arrays):
    return {name: (VMEM, array) for name, array in arrays.items()}


def swap(count, bit):
    return [(i, i ^ bit) for i in range(count)]


def neighbours(low, high, axis):
    count = lax.axis_size(axis)
    before = lax.ppermute(high, axis, [(i, i + 1) for i in range(count - 1)])
    after = lax.ppermute(low, axis, [(i + 1, i) for i in range(count - 1)])
    return before, after


def beside_z(block):
    if lax.axis_size("wa") == 2:
        both = lax.ppermute(block, "wa", swap(2, 1))
        return both, both
    return neighbours(block, block, "wa")


def summed_over(value, axis):
    count = lax.axis_size(axis)
    if count & (count - 1):
        return lax.psum(value, axis)
    bit = 1
    while bit < count:
        value = value + lax.ppermute(value, axis, swap(count, bit))
        bit *= 2
    return value


def over_gy(msg_y, parts, wells):
    if lax.axis_size("gy") == 2:
        got = lax.ppermute(msg_y, "gy", swap(2, 1))
        return msg_y[:wells] + got[:wells], got, got
    low = jnp.concatenate([a[:, 0] for a in parts])
    high = jnp.concatenate([a[:, -1] for a in parts])
    return (summed_over(msg_y[:wells], "gy"), *neighbours(low, high, "gy"))


def over_gx(total, face_a, face_b, parts):
    if lax.axis_size("gx") == 4:
        more1 = lax.ppermute(jnp.concatenate([total, face_a]), "gx", swap(4, 1))
        more2 = lax.ppermute(jnp.concatenate([total, face_b]), "gx", swap(4, 3))
        more3 = lax.ppermute(total, "gx", swap(4, 2))
        return dict(total=total, more1=more1, more2=more2, more3=more3)
    xm, xp = neighbours(
        jnp.concatenate([a[0] for a in parts]), jnp.concatenate([a[-1] for a in parts]), "gx"
    )
    return dict(total=summed_over(total, "gx"), xm=xm, xp=xp)


def local(
    adjoint, permeability, pore_volume, rock_type, rock_table,
    perf_column, perf_owner, perf_slot, observed,
):
    _, nx, ny, nz = adjoint.shape
    rows = perf_column.shape[0]
    own = observed.shape[0]
    wells = own * lax.axis_size("gx") * lax.axis_size("gy")
    cells = (nx, ny, nz)
    phases, ends = (3,) + cells, (3, 2, ny, nz)
    table = rock_table.T
    perf = dict(
        column=perf_column.reshape(1, rows), owner=perf_owner.reshape(1, rows),
        slot=perf_slot.reshape(1, rows),
    )
    moved = dict(perf, observed=observed, perm=permeability, rock=rock_type, adj=adjoint)
    ins = {"table": (SMEM, table)}
    ins.update({name + "_in": (HBM, array) for name, array in moved.items()})
    outs = {
        "msg_y": (VMEM, (wells + 4 * nx, nz), F32),
        "face_a": (VMEM, (4 * ny, nz), F32),
        "face_b": (VMEM, (4 * ny, nz), F32),
    }
    scratch = {name: pltpu.VMEM(a.shape, a.dtype) for name, a in moved.items()}
    scratch["combined"] = pltpu.VMEM((nx * ny, nz), F32)
    scratch["sems"] = pltpu.SemaphoreType.DMA((len(moved),))
    sent = call(first_kernel, ins, outs, scratch, 60)
    pm, pp = beside_z(permeability)
    adj = adjoint
    cost = pl.CostEstimate(flops=1, bytes_accessed=4 * MIB, transcendentals=0)
    for step in range(STEPS):
        first, last = step == 0, step == STEPS - 1
        parts = [adj[p] for p in range(3)]
        total, ym, yp = over_gy(sent.msg_y, parts + [permeability[1]] * first, wells)
        sums = over_gx(total, sent.face_a, sent.face_b, parts + [permeability[0]] * first)
        zm, zp = beside_z(adj)
        ins = in_vmem(adj=adj, ym=ym, yp=yp, zm=zm, zp=zp)
        outs = {"base": (VMEM, phases, F32)}
        if not last:
            outs["flow"] = (VMEM, cells, F32)
        if first:
            ins["table"] = (SMEM, table)
            ins.update(in_vmem(
                perm=permeability, pm=pm, pp=pp, pore=pore_volume, rock=rock_type,
                observed=observed, **perf,
            ))
            outs.update(
                t=(VMEM, (6,) + cells, F32), weight=(VMEM, cells, F32),
                index=(VMEM, cells, F32), gain=(VMEM, phases, F32), mob=(VMEM, ends, F32),
                keep=(VMEM, phases, F32), take=(VMEM, phases, F32), q=(VMEM, phases, F32),
                reply=(VMEM, cells, F32), counts=(VMEM, (wells, nx * ny), BF16),
                counts_t=(VMEM, (nx * ny, wells), BF16),
            )
        else:
            ins.update(in_vmem(
                t=fixed.t, keep=fixed.keep, take=fixed.take, edge_keep=edge.edge_keep,
                edge_take=edge.edge_take,
            ))
            if not last:
                ins.update(in_vmem(gain=fixed.gain))
        inner = call(functools.partial(inner_kernel, first, last), ins, outs, {}, 24, cost)
        if first:
            fixed = inner
        ins = in_vmem(
            **sums, base=inner.base, observed=observed, counts_t=fixed.counts_t,
            index=fixed.index, q=fixed.q,
        )
        if first:
            ins.update(in_vmem(
                perm=permeability, pore=pore_volume, weight=fixed.weight, mob=fixed.mob, adj=adj
            ))
        else:
            ins.update(in_vmem(edge_t=edge.edge_t, edge_take=edge.edge_take))
        if last:
            outs = {"new": (HBM, phases, F32), "sens": (VMEM, (own, nz), F32)}
            scratch = {
                "combined": pltpu.VMEM((wells, nz), F32),
                "held": pltpu.VMEM(phases, F32),
                "sems": pltpu.SemaphoreType.DMA((nx,)),
            }
        else:
            ins.update(in_vmem(
                gain=fixed.gain, flow=inner.flow, reply=fixed.reply, counts=fixed.counts
            ))
            outs = {
                "new": (VMEM, phases, F32),
                "msg_y": (VMEM, (wells + 3 * nx, nz), F32),
                "face_a": (VMEM, (3 * ny, nz), F32),
                "face_b": (VMEM, (3 * ny, nz), F32),
            }
            scratch = {"combined": pltpu.VMEM((nx * ny, nz), F32)}
        if first:
            outs.update(
                edge_t=(VMEM, (2, ny, nz), F32), edge_keep=(VMEM, ends, F32),
                edge_take=(VMEM, ends, F32),
            )
        sent = call(functools.partial(well_kernel, first, last), ins, outs, scratch)
        if first:
            edge = sent
        adj = sent.new
    return (adj, sent.sens)


def solution(mesh):
    cell = P(None, ("members", "gx"), "gy", "wa")
    flat = P(("members", "gx"), "gy", "wa")
    placed = (
        cell, cell, flat, flat, P(), P(("gx", "gy")), P(("gx", "gy"), None), P(("gx", "gy")),
        P(("gx", "gy"), "wa"),
    )
    return jax.shard_map(
        local,
        mesh=mesh,
        in_specs=placed,
        out_specs=(cell, P(("members", "gx", "gy"), "wa")),
        check_vma=False,
    )
```

```python
import functools

import jax
import jax.numpy as jnp
from jax import lax
from jax.experimental import pallas as pl
from jax.experimental.pallas import tpu as pltpu
from jax.sharding import PartitionSpec as P

STEPS = 4
F32 = jnp.float32
BF16 = jnp.bfloat16
VMEM = pl.BlockSpec(memory_space=pltpu.VMEM)
HBM = pl.BlockSpec(memory_space=pltpu.HBM)
SMEM = pl.BlockSpec(memory_space=pltpu.SMEM)
MIB = 1024 * 1024


class Refs(dict):
    __getattr__ = dict.__getitem__


def harmonic(first, second):
    return 2.0 * first * second / (first + second)


def split(value):
    high = value.astype(BF16)
    rest = value - high.astype(F32)
    middle = rest.astype(BF16)
    low = (rest - middle.astype(F32)).astype(BF16)
    return jnp.concatenate([high, middle, low], axis=1)


def counted(counts, value):
    n = value.shape[1]
    out = jnp.dot(counts, split(value), preferred_element_type=F32)
    return out[:, :n] + (out[:, n : 2 * n] + out[:, 2 * n :])


def odd(axis):
    return lax.rem(lax.axis_index(axis), 2) == 1


def own_rows(own):
    owner = lax.axis_index("gx") * lax.axis_size("gy") + lax.axis_index("gy")
    return pl.ds(pl.multiple_of(owner * own, own), own)


def hits(r, wells, own, columns):
    rows = r.column.shape[1]
    well = r.owner[...] * own + r.slot[...]
    well_hit = (lax.broadcasted_iota(jnp.int32, (wells, rows), 0) == well).astype(BF16)
    col_hit = lax.broadcasted_iota(jnp.int32, (columns, rows), 0) == r.column[...]
    return well_hit, col_hit.astype(BF16)


def pairs(first, second):
    out = lax.dot_general(
        first, second, (((1,), (1,)), ((), ())), preferred_element_type=F32
    )
    return out.astype(BF16)


def plane_mobility(r, x):
    kind = r.rock[x]
    root = jnp.sqrt(r.perm[0, x] * r.perm[1, x])
    index = root / (1.0 + root)
    mobility = []
    for p in range(3):
        m = jnp.full(kind.shape, r.table[p, 0], F32)
        for k in range(1, r.table.shape[1]):
            m = jnp.where(kind == k, r.table[p, k], m)
        mobility.append(m)
    return index, mobility


def send_y(r, row, value):
    ny = value.shape[0]
    r.msg_y[row : row + 1, :] = jnp.where(odd("gy"), value[0:1, :], value[ny - 1 : ny, :])


def send_x(r, p, low, high):
    ny = low.shape[0]
    r.face_a[p * ny : (p + 1) * ny, :] = jnp.where(odd("gx"), low, high)
    r.face_b[p * ny : (p + 1) * ny, :] = jnp.where(odd("gx"), high, low)


def first_kernel(names, *refs):
    r = Refs(zip(names, refs))
    moved = ("column", "owner", "slot", "observed", "table", "perm", "rock", "adj")
    copies = {}
    for i, name in enumerate(moved):
        copies[name] = pltpu.make_async_copy(r[name + "_in"], r[name], r.sems.at[i])
        copies[name].start()
    _, nx, ny, nz = r.adj.shape
    own = r.observed.shape[0]
    wells = r.msg_y.shape[0] - 4 * nx
    for name in moved[:4]:
        copies[name].wait()
    well_hit, col_hit = hits(r, wells, own, nx * ny)
    counts = pairs(well_hit, col_hit)
    for name in moved[4:]:
        copies[name].wait()
    for x in range(nx):
        index, mobility = plane_mobility(r, x)
        total = jnp.zeros((ny, nz), F32)
        for p in range(3):
            total = total + mobility[p] * r.adj[p, x]
            send_y(r, wells + p * nx + x, r.adj[p, x])
        send_y(r, wells + 3 * nx + x, r.perm[1, x])
        r.combined[x * ny : (x + 1) * ny, :] = 0.25 * index * total
    for p in range(3):
        send_x(r, p, r.adj[p, 0], r.adj[p, nx - 1])
    send_x(r, 3, r.perm[0, 0], r.perm[0, nx - 1])
    r.msg_y[0:wells, :] = counted(counts, r.combined[...])
    r.msg_y[own_rows(own), :] = r.msg_y[own_rows(own), :] - r.observed[...]


def inner_kernel(first, last, names, *refs):
    r = Refs(zip(names, refs))
    _, nx, ny, nz = r.adj.shape
    lane = lax.broadcasted_iota(jnp.int32, (ny, nz), 1)
    sub = lax.broadcasted_iota(jnp.int32, (ny, nz), 0)
    at_first, at_last = lane == 0, lane == nz - 1
    top, bottom = sub == 0, sub == ny - 1
    y0 = r.ym.shape[0] - (4 if first else 3) * nx

    def y_minus(value, p, x):
        edge = r.ym[y0 + p * nx + x : y0 + p * nx + x + 1, :]
        return jnp.where(top, edge, pltpu.roll(value, 1, 0))

    def y_plus(value, p, x):
        edge = r.yp[y0 + p * nx + x : y0 + p * nx + x + 1, :]
        return jnp.where(bottom, edge, pltpu.roll(value, ny - 1, 0))

    def z_minus(value, beside):
        return pltpu.roll(jnp.where(at_last, beside, value), 1, 1)

    def z_plus(value, beside):
        return pltpu.roll(jnp.where(at_first, beside, value), nz - 1, 1)

    if first:
        own = r.observed.shape[0]
        wells = r.counts.shape[0]
        well_hit, col_hit = hits(r, wells, own, nx * ny)
        r.counts[...] = pairs(well_hit, col_hit)
        r.counts_t[...] = pairs(col_hit, well_hit)
        ends = {a: (lax.axis_index(a) == 0, lax.axis_index(a) == lax.axis_size(a) - 1)
                for a in ("gy", "wa")}
        zero = jnp.zeros((ny, nz), F32)
    for x in range(nx):
        edge = x in (0, nx - 1)
        if first:
            k = r.perm[0, x]
            txm = harmonic(k, r.perm[0, x - 1]) if x else zero
            txp = harmonic(k, r.perm[0, x + 1]) if x < nx - 1 else zero
            k = r.perm[1, x]
            tym = harmonic(k, jnp.where(top & ends["gy"][0], 0.0, y_minus(k, 3, x)))
            typ = harmonic(k, jnp.where(bottom & ends["gy"][1], 0.0, y_plus(k, 3, x)))
            k = r.perm[2, x]
            km, kp = z_minus(k, r.pm[2, x]), z_plus(k, r.pp[2, x])
            tzm = harmonic(k, jnp.where(at_first & ends["wa"][0], 0.0, km))
            tzp = harmonic(k, jnp.where(at_last & ends["wa"][1], 0.0, kp))
            weights = (txm, txp, tym, typ, tzm, tzp)
            for f, t in enumerate(weights):
                r.t[f, x] = t
            weight_sum = txm + txp + tym + typ + tzm + tzp
            r.weight[x] = weight_sum
            pore = r.pore[x]
            index, mobility = plane_mobility(r, x)
            r.index[x] = index
            reply = zero
        else:
            txm, txp, tym, typ, tzm, tzp = (r.t[f, x] for f in range(6))
        flow = jnp.zeros((ny, nz), F32)
        for p in range(3):
            value = r.adj[p, x]
            beside = tym * y_minus(value, p, x) + typ * y_plus(value, p, x)
            beside = beside + tzm * z_minus(value, r.zm[p, x])
            beside = beside + tzp * z_plus(value, r.zp[p, x])
            if x:
                beside = beside + txm * r.adj[p, x - 1]
            if x < nx - 1:
                beside = beside + txp * r.adj[p, x + 1]
            if first:
                m = mobility[p]
                gain = 0.25 * index * m
                r.gain[p, x] = gain
                if edge:
                    r.mob[p, 1 if x else 0] = m
                    r.base[p, x] = beside
                    continue
                inverse = 1.0 / (pore + m * weight_sum)
                keep, take = pore * inverse, m * inverse
                r.keep[p, x] = keep
                r.take[p, x] = take
                q = take * index
                r.q[p, x] = q
                reply = reply + gain * q
            elif edge:
                e = 1 if x else 0
                keep, take = r.edge_keep[p, e], r.edge_take[p, e]
            else:
                keep, take = r.keep[p, x], r.take[p, x]
            base = keep * value + take * beside
            r.base[p, x] = base
            if not last and not edge:
                flow = flow + r.gain[p, x] * base
        if not edge:
            if not last:
                r.flow[x] = flow
            if first:
                r.reply[x] = reply


def well_kernel(first, last, names, *refs):
    r = Refs(zip(names, refs))
    _, nx, ny, nz = r.base.shape
    wells = r.total.shape[0]
    total = r.total[...]
    for name in names:
        if name.startswith("more"):
            total = total + r[name][0:wells, :]
    if last:
        own = r.observed.shape[0]
        r.combined[...] = total
        r.sens_held[...] = r.combined[own_rows(own), :] + r.observed[...]
        copies = [pltpu.make_async_copy(r.sens_held, r.sens, r.sems.at[nx])]
        copies[0].start()
    column_sum = counted(r.counts_t[...], jnp.tanh(total))

    def x_face(p, e):
        if "xm" in r:
            return (r.xp if e else r.xm)[p * ny : (p + 1) * ny, :]
        at = slice(wells + p * ny, wells + (p + 1) * ny)
        one, ring = r.more1[at, :], r.more2[at, :]
        return jnp.where(odd("gx"), ring, one) if e else jnp.where(odd("gx"), one, ring)

    part = 4 if nx % 4 == 0 else 1
    gx, size_x = lax.axis_index("gx"), lax.axis_size("gx")
    for x in range(nx):
        edge = x in (0, nx - 1)
        e = 1 if x else 0
        wells_here = column_sum[x * ny : (x + 1) * ny, :]
        flow = None
        if edge:
            well_term = r.index[x] * wells_here
            if first:
                k = jnp.where(gx == (size_x - 1 if e else 0), 0.0, x_face(3, e))
                tx = harmonic(r.perm[0, x], k)
                r.edge_t[e] = tx
                weight_sum = r.weight[x] + tx
                pore = r.pore[x]
            else:
                tx = r.edge_t[e]
        for p in range(3):
            if not edge:
                new = r.base[p, x] + r.q[p, x] * wells_here
            elif first:
                m = r.mob[p, e]
                inverse = 1.0 / (pore + m * weight_sum)
                keep, take = pore * inverse, m * inverse
                r.edge_keep[p, e] = keep
                r.edge_take[p, e] = take
                beside = r.base[p, x] + tx * x_face(p, e)
                new = keep * r.adj[p, x] + take * (beside + well_term)
            else:
                new = r.base[p, x] + r.edge_take[p, e] * (tx * x_face(p, e) + well_term)
            if last:
                r.held[p, x] = new
                continue
            r.new[p, x] = new
            send_y(r, wells + p * nx + x, new)
            if edge:
                term = r.gain[p, x] * new
                flow = term if flow is None else flow + term
                if x:
                    send_x(r, p, r.new[p, 0], new)
        if last:
            if x % part == part - 1:
                at = pl.ds(x - part + 1, part)
                copies.append(
                    pltpu.make_async_copy(
                        r.held.at[:, at], r.new.at[:, at], r.sems.at[x // part]
                    )
                )
                copies[-1].start()
            continue
        if not edge:
            flow = r.flow[x] + r.reply[x] * wells_here
        r.combined[x * ny : (x + 1) * ny, :] = flow
    if last:
        for copy in copies:
            copy.wait()
    else:
        r.msg_y[0:wells, :] = counted(r.counts[...], r.combined[...])
        own = r.observed.shape[0]
        r.msg_y[own_rows(own), :] = r.msg_y[own_rows(own), :] - r.observed[...]


def call(kernel, ins, outs, scratch, limit=24, cost=None):
    names = tuple(ins) + tuple(outs) + tuple(scratch)
    result = pl.pallas_call(
        functools.partial(kernel, names),
        in_specs=[spec for spec, _ in ins.values()],
        out_specs=[spec for spec, _, _ in outs.values()],
        out_shape=[jax.ShapeDtypeStruct(shape, kind) for _, shape, kind in outs.values()],
        scratch_shapes=list(scratch.values()),
        compiler_params=pltpu.CompilerParams(vmem_limit_bytes=int(limit * MIB)),
        cost_estimate=cost,
    )(*[array for _, array in ins.values()])
    return Refs(zip(outs, result))


def in_vmem(**arrays):
    return {name: (VMEM, array) for name, array in arrays.items()}


def swap(count, bit):
    return [(i, i ^ bit) for i in range(count)]


def neighbours(low, high, axis):
    count = lax.axis_size(axis)
    before = lax.ppermute(high, axis, [(i, i + 1) for i in range(count - 1)])
    after = lax.ppermute(low, axis, [(i + 1, i) for i in range(count - 1)])
    return before, after


def beside_z(block):
    if lax.axis_size("wa") == 2:
        both = lax.ppermute(block, "wa", swap(2, 1))
        return both, both
    return neighbours(block, block, "wa")


def summed_over(value, axis):
    count = lax.axis_size(axis)
    if count & (count - 1):
        return lax.psum(value, axis)
    bit = 1
    while bit < count:
        value = value + lax.ppermute(value, axis, swap(count, bit))
        bit *= 2
    return value


def over_gy(msg_y, parts, wells):
    if lax.axis_size("gy") == 2:
        got = lax.ppermute(msg_y, "gy", swap(2, 1))
        return msg_y[:wells] + got[:wells], got, got
    low = jnp.concatenate([a[:, 0] for a in parts])
    high = jnp.concatenate([a[:, -1] for a in parts])
    return (summed_over(msg_y[:wells], "gy"), *neighbours(low, high, "gy"))


def over_gx(total, face_a, face_b, parts):
    if lax.axis_size("gx") == 4:
        more1 = lax.ppermute(jnp.concatenate([total, face_a]), "gx", swap(4, 1))
        more2 = lax.ppermute(jnp.concatenate([total, face_b]), "gx", swap(4, 3))
        more3 = lax.ppermute(total, "gx", swap(4, 2))
        return dict(total=total, more1=more1, more2=more2, more3=more3)
    xm, xp = neighbours(
        jnp.concatenate([a[0] for a in parts]), jnp.concatenate([a[-1] for a in parts]), "gx"
    )
    return dict(total=summed_over(total, "gx"), xm=xm, xp=xp)


def local(
    adjoint, permeability, pore_volume, rock_type, rock_table,
    perf_column, perf_owner, perf_slot, observed,
):
    _, nx, ny, nz = adjoint.shape
    rows = perf_column.shape[0]
    own = observed.shape[0]
    wells = own * lax.axis_size("gx") * lax.axis_size("gy")
    cells = (nx, ny, nz)
    phases, ends = (3,) + cells, (3, 2, ny, nz)
    table = rock_table.T
    perf = dict(
        column=perf_column.reshape(1, rows), owner=perf_owner.reshape(1, rows),
        slot=perf_slot.reshape(1, rows),
    )
    moved = dict(perf, observed=observed, perm=permeability, rock=rock_type, adj=adjoint, table=table)
    ins = {name + "_in": (HBM, array) for name, array in moved.items()}
    outs = {
        "msg_y": (VMEM, (wells + 4 * nx, nz), F32),
        "face_a": (VMEM, (4 * ny, nz), F32),
        "face_b": (VMEM, (4 * ny, nz), F32),
    }
    scratch = {name: pltpu.VMEM(a.shape, a.dtype) for name, a in moved.items()}
    scratch["table"] = pltpu.SMEM(table.shape, F32)
    scratch["combined"] = pltpu.VMEM((nx * ny, nz), F32)
    scratch["sems"] = pltpu.SemaphoreType.DMA((len(moved),))
    sent = call(first_kernel, ins, outs, scratch, 53.75)
    pm, pp = beside_z(permeability)
    adj = adjoint
    cost = pl.CostEstimate(flops=1, bytes_accessed=4 * MIB, transcendentals=0)
    for step in range(STEPS):
        first, last = step == 0, step == STEPS - 1
        parts = [adj[p] for p in range(3)]
        total, ym, yp = over_gy(sent.msg_y, parts + [permeability[1]] * first, wells)
        sums = over_gx(total, sent.face_a, sent.face_b, parts + [permeability[0]] * first)
        zm, zp = beside_z(adj)
        ins = in_vmem(adj=adj, ym=ym, yp=yp, zm=zm, zp=zp)
        outs = {"base": (VMEM, phases, F32)}
        if not last:
            outs["flow"] = (VMEM, cells, F32)
        if first:
            ins["table"] = (SMEM, table)
            ins.update(in_vmem(
                perm=permeability, pm=pm, pp=pp, pore=pore_volume, rock=rock_type,
                observed=observed, **perf,
            ))
            outs.update(
                t=(VMEM, (6,) + cells, F32), weight=(VMEM, cells, F32),
                index=(VMEM, cells, F32), gain=(VMEM, phases, F32), mob=(VMEM, ends, F32),
                keep=(VMEM, phases, F32), take=(VMEM, phases, F32), q=(VMEM, phases, F32),
                reply=(VMEM, cells, F32), counts=(VMEM, (wells, nx * ny), BF16),
                counts_t=(VMEM, (nx * ny, wells), BF16),
            )
        else:
            ins.update(in_vmem(
                t=fixed.t, keep=fixed.keep, take=fixed.take, edge_keep=edge.edge_keep,
                edge_take=edge.edge_take,
            ))
            if not last:
                ins.update(in_vmem(gain=fixed.gain))
        inner = call(functools.partial(inner_kernel, first, last), ins, outs, {}, 24, cost)
        if first:
            fixed = inner
        ins = in_vmem(
            **sums, base=inner.base, observed=observed, counts_t=fixed.counts_t,
            index=fixed.index, q=fixed.q,
        )
        if first:
            ins.update(in_vmem(
                perm=permeability, pore=pore_volume, weight=fixed.weight, mob=fixed.mob, adj=adj
            ))
        else:
            ins.update(in_vmem(edge_t=edge.edge_t, edge_take=edge.edge_take))
        if last:
            outs = {"new": (HBM, phases, F32), "sens": (HBM, (own, nz), F32)}
            scratch = {
                "combined": pltpu.VMEM((wells, nz), F32),
                "held": pltpu.VMEM(phases, F32),
                "sens_held": pltpu.VMEM((own, nz), F32),
                "sems": pltpu.SemaphoreType.DMA((nx + 1,)),
            }
        else:
            ins.update(in_vmem(
                gain=fixed.gain, flow=inner.flow, reply=fixed.reply, counts=fixed.counts
            ))
            outs = {
                "new": (VMEM, phases, F32),
                "msg_y": (VMEM, (wells + 3 * nx, nz), F32),
                "face_a": (VMEM, (3 * ny, nz), F32),
                "face_b": (VMEM, (3 * ny, nz), F32),
            }
            scratch = {"combined": pltpu.VMEM((nx * ny, nz), F32)}
        if first:
            outs.update(
                edge_t=(VMEM, (2, ny, nz), F32), edge_keep=(VMEM, ends, F32),
                edge_take=(VMEM, ends, F32),
            )
        sent = call(functools.partial(well_kernel, first, last), ins, outs, scratch)
        if first:
            edge = sent
        adj = sent.new
    return (adj, sent.sens)


def solution(mesh):
    cell = P(None, ("members", "gx"), "gy", "wa")
    flat = P(("members", "gx"), "gy", "wa")
    placed = (
        cell, cell, flat, flat, P(), P(("gx", "gy")), P(("gx", "gy"), None), P(("gx", "gy")),
        P(("gx", "gy"), "wa"),
    )
    return jax.shard_map(
        local,
        mesh=mesh,
        in_specs=placed,
        out_specs=(cell, P(("members", "gx", "gy"), "wa")),
        check_vma=False,
    )
```

```python
import functools

import jax
import jax.numpy as jnp
from jax import lax
from jax.experimental import pallas as pl
from jax.experimental.pallas import tpu as pltpu
from jax.sharding import PartitionSpec as P

STEPS = 4
F32 = jnp.float32
BF16 = jnp.bfloat16
VMEM = pl.BlockSpec(memory_space=pltpu.VMEM)
HBM = pl.BlockSpec(memory_space=pltpu.HBM)
SMEM = pl.BlockSpec(memory_space=pltpu.SMEM)
MIB = 1024 * 1024


class Refs(dict):
    __getattr__ = dict.__getitem__


def harmonic(first, second):
    return 2.0 * first * second / (first + second)


def split(value):
    high = value.astype(BF16)
    rest = value - high.astype(F32)
    middle = rest.astype(BF16)
    low = (rest - middle.astype(F32)).astype(BF16)
    return jnp.concatenate([high, middle, low], axis=1)


def counted(counts, value):
    n = value.shape[1]
    out = jnp.dot(counts, split(value), preferred_element_type=F32)
    return out[:, :n] + (out[:, n : 2 * n] + out[:, 2 * n :])


def odd(axis):
    return lax.rem(lax.axis_index(axis), 2) == 1


def own_rows(own):
    owner = lax.axis_index("gx") * lax.axis_size("gy") + lax.axis_index("gy")
    return pl.ds(pl.multiple_of(owner * own, own), own)


def hits(r, wells, own, columns):
    rows = r.column.shape[1]
    well = r.owner[...] * own + r.slot[...]
    well_hit = (lax.broadcasted_iota(jnp.int32, (wells, rows), 0) == well).astype(BF16)
    col_hit = lax.broadcasted_iota(jnp.int32, (columns, rows), 0) == r.column[...]
    return well_hit, col_hit.astype(BF16)


def pairs(first, second):
    out = lax.dot_general(
        first, second, (((1,), (1,)), ((), ())), preferred_element_type=F32
    )
    return out.astype(BF16)


def plane_mobility(r, x):
    kind = r.rock[x]
    root = jnp.sqrt(r.perm[0, x] * r.perm[1, x])
    index = root / (1.0 + root)
    mobility = []
    for p in range(3):
        m = jnp.full(kind.shape, r.table[p, 0], F32)
        for k in range(1, r.table.shape[1]):
            m = jnp.where(kind == k, r.table[p, k], m)
        mobility.append(m)
    return index, mobility


def send_y(r, row, value):
    ny = value.shape[0]
    r.msg_y[row : row + 1, :] = jnp.where(odd("gy"), value[0:1, :], value[ny - 1 : ny, :])


def send_x(r, p, low, high):
    ny = low.shape[0]
    r.face_a[p * ny : (p + 1) * ny, :] = jnp.where(odd("gx"), low, high)
    r.face_b[p * ny : (p + 1) * ny, :] = jnp.where(odd("gx"), high, low)


def first_kernel(names, *refs):
    r = Refs(zip(names, refs))
    moved = ("column", "owner", "slot", "observed", "table", "perm", "rock", "adj")
    copies = {}
    for i, name in enumerate(moved):
        copies[name] = pltpu.make_async_copy(r[name + "_in"], r[name], r.sems.at[i])
        copies[name].start()
    _, nx, ny, nz = r.adj.shape
    own = r.observed.shape[0]
    wells = r.msg_y.shape[0] - 4 * nx
    for name in moved[:4]:
        copies[name].wait()
    well_hit, col_hit = hits(r, wells, own, nx * ny)
    counts = pairs(well_hit, col_hit)
    for name in moved[4:]:
        copies[name].wait()
    for x in range(nx):
        index, mobility = plane_mobility(r, x)
        total = jnp.zeros((ny, nz), F32)
        for p in range(3):
            total = total + mobility[p] * r.adj[p, x]
            send_y(r, wells + p * nx + x, r.adj[p, x])
        send_y(r, wells + 3 * nx + x, r.perm[1, x])
        r.combined[x * ny : (x + 1) * ny, :] = 0.25 * index * total
    for p in range(3):
        send_x(r, p, r.adj[p, 0], r.adj[p, nx - 1])
    send_x(r, 3, r.perm[0, 0], r.perm[0, nx - 1])
    r.msg_y[0:wells, :] = counted(counts, r.combined[...])
    r.msg_y[own_rows(own), :] = r.msg_y[own_rows(own), :] - r.observed[...]


def inner_kernel(first, last, names, *refs):
    r = Refs(zip(names, refs))
    _, nx, ny, nz = r.adj.shape
    lane = lax.broadcasted_iota(jnp.int32, (ny, nz), 1)
    sub = lax.broadcasted_iota(jnp.int32, (ny, nz), 0)
    at_first, at_last = lane == 0, lane == nz - 1
    top, bottom = sub == 0, sub == ny - 1
    y0 = r.ym.shape[0] - (4 if first else 3) * nx

    def y_minus(value, p, x):
        edge = r.ym[y0 + p * nx + x : y0 + p * nx + x + 1, :]
        return jnp.where(top, edge, pltpu.roll(value, 1, 0))

    def y_plus(value, p, x):
        edge = r.yp[y0 + p * nx + x : y0 + p * nx + x + 1, :]
        return jnp.where(bottom, edge, pltpu.roll(value, ny - 1, 0))

    def z_minus(value, beside):
        return pltpu.roll(jnp.where(at_last, beside, value), 1, 1)

    def z_plus(value, beside):
        return pltpu.roll(jnp.where(at_first, beside, value), nz - 1, 1)

    if first:
        own = r.observed.shape[0]
        wells = r.counts.shape[0]
        well_hit, col_hit = hits(r, wells, own, nx * ny)
        r.counts[...] = pairs(well_hit, col_hit)
        r.counts_t[...] = pairs(col_hit, well_hit)
        ends = {a: (lax.axis_index(a) == 0, lax.axis_index(a) == lax.axis_size(a) - 1)
                for a in ("gy", "wa")}
        zero = jnp.zeros((ny, nz), F32)
    for x in range(nx):
        edge = x in (0, nx - 1)
        if first:
            k = r.perm[0, x]
            txm = harmonic(k, r.perm[0, x - 1]) if x else zero
            txp = harmonic(k, r.perm[0, x + 1]) if x < nx - 1 else zero
            k = r.perm[1, x]
            tym = harmonic(k, jnp.where(top & ends["gy"][0], 0.0, y_minus(k, 3, x)))
            typ = harmonic(k, jnp.where(bottom & ends["gy"][1], 0.0, y_plus(k, 3, x)))
            k = r.perm[2, x]
            km, kp = z_minus(k, r.pm[2, x]), z_plus(k, r.pp[2, x])
            tzm = harmonic(k, jnp.where(at_first & ends["wa"][0], 0.0, km))
            tzp = harmonic(k, jnp.where(at_last & ends["wa"][1], 0.0, kp))
            weights = (txm, txp, tym, typ, tzm, tzp)
            for f, t in enumerate(weights):
                r.t[f, x] = t
            weight_sum = txm + txp + tym + typ + tzm + tzp
            r.weight[x] = weight_sum
            pore = r.pore[x]
            index, mobility = plane_mobility(r, x)
            r.index[x] = index
            reply = zero
        else:
            txm, txp, tym, typ, tzm, tzp = (r.t[f, x] for f in range(6))
        flow = jnp.zeros((ny, nz), F32)
        for p in range(3):
            value = r.adj[p, x]
            beside = tym * y_minus(value, p, x) + typ * y_plus(value, p, x)
            beside = beside + tzm * z_minus(value, r.zm[p, x])
            beside = beside + tzp * z_plus(value, r.zp[p, x])
            if x:
                beside = beside + txm * r.adj[p, x - 1]
            if x < nx - 1:
                beside = beside + txp * r.adj[p, x + 1]
            if first:
                m = mobility[p]
                gain = 0.25 * index * m
                r.gain[p, x] = gain
                if edge:
                    r.mob[p, 1 if x else 0] = m
                    r.base[p, x] = beside
                    continue
                inverse = 1.0 / (pore + m * weight_sum)
                keep, take = pore * inverse, m * inverse
                r.keep[p, x] = keep
                r.take[p, x] = take
                q = take * index
                r.q[p, x] = q
                reply = reply + gain * q
            elif edge:
                e = 1 if x else 0
                keep, take = r.edge_keep[p, e], r.edge_take[p, e]
            else:
                keep, take = r.keep[p, x], r.take[p, x]
            base = keep * value + take * beside
            r.base[p, x] = base
            if not last and not edge:
                flow = flow + r.gain[p, x] * base
        if not edge:
            if not last:
                r.flow[x] = flow
            if first:
                r.reply[x] = reply


def well_kernel(first, last, names, *refs):
    r = Refs(zip(names, refs))
    _, nx, ny, nz = r.base.shape
    wells = r.total.shape[0]
    total = r.total[...]
    for name in names:
        if name.startswith("more"):
            total = total + r[name][0:wells, :]
    if last:
        own = r.observed.shape[0]
        r.combined[...] = total
        r.sens_held[...] = r.combined[own_rows(own), :] + r.observed[...]
        copies = [pltpu.make_async_copy(r.sens_held, r.sens, r.sems.at[nx])]
        copies[0].start()
    column_sum = counted(r.counts_t[...], jnp.tanh(total))

    def x_face(p, e):
        if "xm" in r:
            return (r.xp if e else r.xm)[p * ny : (p + 1) * ny, :]
        at = slice(wells + p * ny, wells + (p + 1) * ny)
        one, ring = r.more1[at, :], r.more2[at, :]
        return jnp.where(odd("gx"), ring, one) if e else jnp.where(odd("gx"), one, ring)

    part = 4 if nx % 4 == 0 else 1
    gx, size_x = lax.axis_index("gx"), lax.axis_size("gx")
    for x in range(nx):
        edge = x in (0, nx - 1)
        e = 1 if x else 0
        wells_here = column_sum[x * ny : (x + 1) * ny, :]
        flow = None
        if edge:
            well_term = r.index[x] * wells_here
            if first:
                k = jnp.where(gx == (size_x - 1 if e else 0), 0.0, x_face(3, e))
                tx = harmonic(r.perm[0, x], k)
                r.edge_t[e] = tx
                weight_sum = r.weight[x] + tx
                pore = r.pore[x]
            else:
                tx = r.edge_t[e]
        for p in range(3):
            if not edge:
                new = r.base[p, x] + r.q[p, x] * wells_here
            elif first:
                m = r.mob[p, e]
                inverse = 1.0 / (pore + m * weight_sum)
                keep, take = pore * inverse, m * inverse
                r.edge_keep[p, e] = keep
                r.edge_take[p, e] = take
                beside = r.base[p, x] + tx * x_face(p, e)
                new = keep * r.adj[p, x] + take * (beside + well_term)
            else:
                new = r.base[p, x] + r.edge_take[p, e] * (tx * x_face(p, e) + well_term)
            if last:
                r.held[p, x] = new
                continue
            r.new[p, x] = new
            send_y(r, wells + p * nx + x, new)
            if edge:
                term = r.gain[p, x] * new
                flow = term if flow is None else flow + term
                if x:
                    send_x(r, p, r.new[p, 0], new)
        if last:
            if x % part == part - 1:
                at = pl.ds(x - part + 1, part)
                copies.append(
                    pltpu.make_async_copy(
                        r.held.at[:, at], r.new.at[:, at], r.sems.at[x // part]
                    )
                )
                copies[-1].start()
            continue
        if not edge:
            flow = r.flow[x] + r.reply[x] * wells_here
        r.combined[x * ny : (x + 1) * ny, :] = flow
    if last:
        for copy in copies:
            copy.wait()
    else:
        r.msg_y[0:wells, :] = counted(r.counts[...], r.combined[...])
        own = r.observed.shape[0]
        r.msg_y[own_rows(own), :] = r.msg_y[own_rows(own), :] - r.observed[...]


def call(kernel, ins, outs, scratch, limit=24, cost=None):
    names = tuple(ins) + tuple(outs) + tuple(scratch)
    result = pl.pallas_call(
        functools.partial(kernel, names),
        in_specs=[spec for spec, _ in ins.values()],
        out_specs=[spec for spec, _, _ in outs.values()],
        out_shape=[jax.ShapeDtypeStruct(shape, kind) for _, shape, kind in outs.values()],
        scratch_shapes=list(scratch.values()),
        compiler_params=pltpu.CompilerParams(vmem_limit_bytes=int(limit * MIB)),
        cost_estimate=cost,
    )(*[array for _, array in ins.values()])
    return Refs(zip(outs, result))


def in_vmem(**arrays):
    return {name: (VMEM, array) for name, array in arrays.items()}


def swap(count, bit):
    return [(i, i ^ bit) for i in range(count)]


def neighbours(low, high, axis):
    count = lax.axis_size(axis)
    before = lax.ppermute(high, axis, [(i, i + 1) for i in range(count - 1)])
    after = lax.ppermute(low, axis, [(i + 1, i) for i in range(count - 1)])
    return before, after


def beside_z(block):
    if lax.axis_size("wa") == 2:
        both = lax.ppermute(block, "wa", swap(2, 1))
        return both, both
    return neighbours(block, block, "wa")


def summed_over(value, axis):
    count = lax.axis_size(axis)
    if count & (count - 1):
        return lax.psum(value, axis)
    bit = 1
    while bit < count:
        value = value + lax.ppermute(value, axis, swap(count, bit))
        bit *= 2
    return value


def over_gy(msg_y, parts, wells):
    if lax.axis_size("gy") == 2:
        got = lax.ppermute(msg_y, "gy", swap(2, 1))
        return msg_y[:wells] + got[:wells], got, got
    low = jnp.concatenate([a[:, 0] for a in parts])
    high = jnp.concatenate([a[:, -1] for a in parts])
    return (summed_over(msg_y[:wells], "gy"), *neighbours(low, high, "gy"))


def over_gx(total, face_a, face_b, parts):
    if lax.axis_size("gx") == 4:
        more1 = lax.ppermute(jnp.concatenate([total, face_a]), "gx", swap(4, 1))
        more2 = lax.ppermute(jnp.concatenate([total, face_b]), "gx", swap(4, 3))
        more3 = lax.ppermute(total, "gx", swap(4, 2))
        return dict(more2=more2, more3=more3, more1=more1, total=total)
    xm, xp = neighbours(
        jnp.concatenate([a[0] for a in parts]), jnp.concatenate([a[-1] for a in parts]), "gx"
    )
    return dict(total=summed_over(total, "gx"), xm=xm, xp=xp)


def local(
    adjoint, permeability, pore_volume, rock_type, rock_table,
    perf_column, perf_owner, perf_slot, observed,
):
    _, nx, ny, nz = adjoint.shape
    rows = perf_column.shape[0]
    own = observed.shape[0]
    wells = own * lax.axis_size("gx") * lax.axis_size("gy")
    cells = (nx, ny, nz)
    phases, ends = (3,) + cells, (3, 2, ny, nz)
    table = rock_table.T
    perf = dict(
        column=perf_column.reshape(1, rows), owner=perf_owner.reshape(1, rows),
        slot=perf_slot.reshape(1, rows),
    )
    moved = dict(perf, observed=observed, perm=permeability, rock=rock_type, adj=adjoint, table=table)
    ins = {name + "_in": (HBM, array) for name, array in moved.items()}
    outs = {
        "msg_y": (VMEM, (wells + 4 * nx, nz), F32),
        "face_a": (VMEM, (4 * ny, nz), F32),
        "face_b": (VMEM, (4 * ny, nz), F32),
    }
    scratch = {name: pltpu.VMEM(a.shape, a.dtype) for name, a in moved.items()}
    scratch["table"] = pltpu.SMEM(table.shape, F32)
    scratch["combined"] = pltpu.VMEM((nx * ny, nz), F32)
    scratch["sems"] = pltpu.SemaphoreType.DMA((len(moved),))
    sent = call(first_kernel, ins, outs, scratch, 53.75)
    pm, pp = beside_z(permeability)
    adj = adjoint
    cost = pl.CostEstimate(flops=1, bytes_accessed=4 * MIB, transcendentals=0)
    for step in range(STEPS):
        first, last = step == 0, step == STEPS - 1
        parts = [adj[p] for p in range(3)]
        total, ym, yp = over_gy(sent.msg_y, parts + [permeability[1]] * first, wells)
        sums = over_gx(total, sent.face_a, sent.face_b, parts + [permeability[0]] * first)
        zm, zp = beside_z(adj)
        ins = in_vmem(adj=adj, ym=ym, yp=yp, zm=zm, zp=zp)
        outs = {"base": (VMEM, phases, F32)}
        if not last:
            outs["flow"] = (VMEM, cells, F32)
        if first:
            ins["table"] = (SMEM, table)
            ins.update(in_vmem(
                perm=permeability, pm=pm, pp=pp, pore=pore_volume, rock=rock_type,
                observed=observed, **perf,
            ))
            outs.update(
                t=(VMEM, (6,) + cells, F32), weight=(VMEM, cells, F32),
                index=(VMEM, cells, F32), gain=(VMEM, phases, F32), mob=(VMEM, ends, F32),
                keep=(VMEM, phases, F32), take=(VMEM, phases, F32), q=(VMEM, phases, F32),
                reply=(VMEM, cells, F32), counts=(VMEM, (wells, nx * ny), BF16),
                counts_t=(VMEM, (nx * ny, wells), BF16),
            )
        else:
            ins.update(in_vmem(
                t=fixed.t, keep=fixed.keep, take=fixed.take, edge_keep=edge.edge_keep,
                edge_take=edge.edge_take,
            ))
            if not last:
                ins.update(in_vmem(gain=fixed.gain))
        inner = call(functools.partial(inner_kernel, first, last), ins, outs, {}, 24, cost)
        if first:
            fixed = inner
        ins = in_vmem(
            **sums, base=inner.base, observed=observed, counts_t=fixed.counts_t,
            index=fixed.index, q=fixed.q,
        )
        if first:
            ins.update(in_vmem(
                perm=permeability, pore=pore_volume, weight=fixed.weight, mob=fixed.mob, adj=adj
            ))
        else:
            ins.update(in_vmem(edge_t=edge.edge_t, edge_take=edge.edge_take))
        if last:
            outs = {"new": (HBM, phases, F32), "sens": (HBM, (own, nz), F32)}
            scratch = {
                "combined": pltpu.VMEM((wells, nz), F32),
                "held": pltpu.VMEM(phases, F32),
                "sens_held": pltpu.VMEM((own, nz), F32),
                "sems": pltpu.SemaphoreType.DMA((nx + 1,)),
            }
        else:
            ins.update(in_vmem(
                gain=fixed.gain, flow=inner.flow, reply=fixed.reply, counts=fixed.counts
            ))
            outs = {
                "new": (VMEM, phases, F32),
                "msg_y": (VMEM, (wells + 3 * nx, nz), F32),
                "face_a": (VMEM, (3 * ny, nz), F32),
                "face_b": (VMEM, (3 * ny, nz), F32),
            }
            scratch = {"combined": pltpu.VMEM((nx * ny, nz), F32)}
        if first:
            outs.update(
                edge_t=(VMEM, (2, ny, nz), F32), edge_keep=(VMEM, ends, F32),
                edge_take=(VMEM, ends, F32),
            )
        sent = call(functools.partial(well_kernel, first, last), ins, outs, scratch)
        if first:
            edge = sent
        adj = sent.new
    return (adj, sent.sens)


def solution(mesh):
    cell = P(None, ("members", "gx"), "gy", "wa")
    flat = P(("members", "gx"), "gy", "wa")
    placed = (
        cell, cell, flat, flat, P(), P(("gx", "gy")), P(("gx", "gy"), None), P(("gx", "gy")),
        P(("gx", "gy"), "wa"),
    )
    return jax.shard_map(
        local,
        mesh=mesh,
        in_specs=placed,
        out_specs=(cell, P(("members", "gx", "gy"), "wa")),
        check_vma=False,
    )
```
